768 devices in a mesh: occ: 12 (over z), tens: 64 (over y, x, core).
Axes of the slice: x: 4, y: 8, z: 12, core: 2. Of those that a mesh axis runs over, the one named last changes fastest.
Arguments:
- tensor: bfloat16 [512, 768, 768], P('tens'), may hold values from -6 to 6
- occ_green: bfloat16 [768, 768], P('occ'), may hold values from -0.21875 to 0.21875
- virt_green: bfloat16 [768, 768], replicated, may hold values from -0.21875 to 0.21875
- tensor_mask: int32 [12, 12], replicated, may hold values from 0 to 1, as said below
- occ_mask: int32 [12, 12], replicated, may hold values from 0 to 1, as said below
- virt_mask: int32 [12, 12], replicated, may hold values from 0 to 1, as said below
Outputs:
- chi: float32 [512, 512], P('tens')
The draws below stay inside these ranges and needn't reach their ends.
Inputs may be any that keep to these rules, and one draw needn't show every extreme that they name: `tensor_mask`: 1 keeps the 64 x 64 block, 0 zeroes it; diagonal blocks are always kept. `occ_mask`: 1 keeps the 64 x 64 block, 0 zeroes it; diagonal blocks are always kept. `virt_mask`: 1 keeps the 64 x 64 block, 0 zeroes it; diagonal blocks are always kept.
All inputs are finite; a program needn't handle non-finite values.
Results may differ from the reference program's by a relative error of at most 0.0041.
Values may be sent and summed in bfloat16 or wider, within the bound.
No kernel may reach another device: no remote copies, remote signals or barrier semaphores. Data moves between devices by JAX's collectives and lax.ppermute only.
A program may use at most 64 MiB of HBM per device.

```python
import jax
import jax.numpy as jnp
from jax import lax

BLOCK = 64
NA = 768
NAB = 12
P_SIZE = 512


def block_pattern(key):
    random_bits = jax.random.randint(key, (NAB, NAB), 0, 2).astype(jnp.int32)
    diagonal_ones = jnp.eye(NAB, dtype=jnp.int32)
    return jnp.maximum(random_bits, diagonal_ones)


def draw_tensor_mask(key, part):
    key = jax.random.fold_in(key, 11)
    return block_pattern(key)


def draw_occ_mask(key, part):
    key = jax.random.fold_in(key, 23)
    return block_pattern(key)


def draw_virt_mask(key, part):
    key = jax.random.fold_in(key, 37)
    return block_pattern(key)


def levels(stream_key, dims, shards, smallest, largest):
    factor_of = 1.0
    for position, parts in shards:
        heights = jax.random.uniform(jax.random.fold_in(jax.random.fold_in(stream_key, 6), position), (parts,), jnp.float32, smallest / len(shards), largest / len(shards))
        factor_of = factor_of * jnp.repeat(jnp.exp(heights), dims[position] // parts).reshape((-1,) + (1,) * (len(dims) - 1 - position))
    return factor_of


def scatter_about(key, extent, scale, reach, shards=(), held_as=jnp.bfloat16):
    drawn = scale * jax.random.normal(key, extent, jnp.float32)
    if shards:
        drawn = drawn * levels(key, extent, shards, -0.22, 0.18)
    return jnp.clip(drawn, -reach, reach).astype(held_as)


def setup_inputs(seed: int = 0) -> dict:
    keys = jax.random.split(jax.random.key(seed), 7)
    return {
        "tensor": scatter_about(keys[0], (P_SIZE, NA, NA), 1.0, 6.0, ((0, 64),)),
        "occ_green": scatter_about(keys[1], (NA, NA), NA ** -0.5, 0.21875, ((0, 12),)),
        "virt_green": scatter_about(keys[2], (NA, NA), NA ** -0.5, 0.21875),
        "tensor_mask": draw_tensor_mask(jax.random.fold_in(keys[6], 71), 0),
        "occ_mask": draw_occ_mask(jax.random.fold_in(keys[6], 71), 0),
        "virt_mask": draw_virt_mask(jax.random.fold_in(keys[6], 71), 0),
    }


def expand(pattern, block_width):
    return jnp.repeat(jnp.repeat(pattern, block_width, axis=0), block_width, axis=1)


def reference(tensor, occ_green, virt_green, tensor_mask, occ_mask, virt_mask):
    tensor_keep = expand(tensor_mask, BLOCK).astype(tensor.dtype)
    masked = tensor * tensor_keep[None]
    occ_part = occ_green * expand(occ_mask, BLOCK).astype(occ_green.dtype)
    virt_part = virt_green * expand(virt_mask, BLOCK).astype(virt_green.dtype)

    def per_function(slice_ri):
        occ_half = jnp.dot(occ_part, slice_ri, preferred_element_type=jnp.float32).astype(tensor.dtype)
        return jnp.dot(occ_half, virt_part, preferred_element_type=jnp.float32).astype(tensor.dtype)

    screened = lax.map(per_function, masked)
    flat_screened = screened.reshape(P_SIZE, NA * NA)
    flat_masked = masked.reshape(P_SIZE, NA * NA)
    chi_total = jnp.dot(flat_screened, flat_masked.T, preferred_element_type=jnp.float32)
    return -chi_total / NA
```

```python
import jax
import jax.numpy as jnp
from jax import lax
from jax.sharding import PartitionSpec as P

BLOCK = 64


def expand(pattern, block_width):
    return jnp.repeat(jnp.repeat(pattern, block_width, axis=0), block_width, axis=1)


def body(tensor, occ_green, virt_green, tensor_mask, occ_mask, virt_mask):
    rows_batch, ao_count = occ_green.shape
    local_ri = tensor.shape[0]
    batches = lax.axis_size("occ")
    cells = lax.axis_size("tens")
    chips = cells // 2
    same_core = [[2 * chip + core for chip in range(chips)] for core in range(2)]
    other_core = [(cell, cell ^ 1) for cell in range(cells)]
    bf16 = jnp.bfloat16
    occ_index = lax.axis_index("occ")
    core = lax.axis_index("tens") % 2
    first_row = occ_index * rows_batch
    per_chip = rows_batch * ao_count // chips

    def regroup(rows):
        message = rows.reshape(local_ri, chips, per_chip).transpose(1, 0, 2)
        moved = lax.all_to_all(
            message, "tens", 0, 0, axis_index_groups=same_core, tiled=True
        )
        return moved.reshape(chips * local_ri, per_chip)

    rows = lax.dynamic_slice_in_dim(tensor, first_row, rows_batch, 1)
    row_pattern = lax.dynamic_slice_in_dim(tensor_mask, occ_index, 1, 0)[0]
    rows = rows * jnp.repeat(row_pattern, BLOCK).astype(bf16)[None, None]
    with jax.named_scope("rows"):
        moved_rows = regroup(rows)

    masked = tensor * expand(tensor_mask, BLOCK).astype(bf16)[None]
    occ_pattern = lax.dynamic_slice_in_dim(occ_mask, occ_index, 1, 0)[0]
    occ_part = occ_green * jnp.repeat(occ_pattern, BLOCK).astype(bf16)[None]
    virt_part = virt_green * expand(virt_mask, BLOCK).astype(bf16)
    occ_half = jnp.einsum(
        "im,pmn->pin", occ_part, masked, preferred_element_type=jnp.float32
    ).astype(bf16)
    screened = jnp.dot(
        occ_half.reshape(local_ri * rows_batch, ao_count),
        virt_part,
        preferred_element_type=jnp.float32,
    ).astype(bf16)
    with jax.named_scope("other_rows"):
        sibling_rows = lax.ppermute(moved_rows, "tens", other_core)
    with jax.named_scope("screened"):
        moved_screened = regroup(screened.reshape(local_ri, rows_batch, ao_count))
    own = moved_rows.reshape(chips, 1, local_ri, per_chip)
    other = sibling_rows.reshape(chips, 1, local_ri, per_chip)
    first = jnp.where(core == 0, own, other)
    second = jnp.where(core == 0, other, own)
    all_rows = jnp.concatenate([first, second], axis=1).reshape(2 * chips * local_ri, per_chip)
    partial_value = lax.dot_general(
        moved_screened, all_rows, (((1,), (1,)), ((), ())), preferred_element_type=jnp.float32
    ).astype(bf16)
    with jax.named_scope("over_plane"):
        shares = lax.all_to_all(
            partial_value.reshape(chips, local_ri, -1),
            "tens",
            0,
            0,
            axis_index_groups=same_core,
            tiled=True,
        )
    batch_share = jnp.sum(shares.astype(jnp.float32), axis=0)
    copies = jnp.broadcast_to(batch_share[None], (batches,) + batch_share.shape)
    with jax.named_scope("over_batches"):
        batch_shares = lax.all_to_all(copies, "occ", 0, 0, tiled=True)
    return jnp.sum(batch_shares, axis=0) * (-1.0 / ao_count)


def solution(mesh):
    in_specs = (P("tens", None, None), P("occ", None), P(), P(), P(), P())
    out_specs = P("tens", None)
    return jax.shard_map(body, mesh=mesh, in_specs=in_specs, out_specs=out_specs, check_vma=False)
```

```python
import jax
import jax.numpy as jnp
from jax import lax
from jax.experimental import pallas as pl
from jax.experimental.pallas import tpu as pltpu
from jax.sharding import PartitionSpec as P

BLOCK = 64
LANES = 128
BF16 = jnp.bfloat16
F32 = jnp.float32


def block_of(size, blocks):
    position = lax.broadcasted_iota(jnp.int32, (size, blocks), 0)
    start = lax.broadcasted_iota(jnp.int32, (size, blocks), 1) * BLOCK
    return ((position >= start) & (position < start + BLOCK)).astype(BF16)


def dot(a, b):
    return jnp.dot(a, b, preferred_element_type=F32)


def dot_t(a, b):
    return lax.dot_general(a, b, (((1,), (1,)), ((), ())), preferred_element_type=F32)


def as_bf16(pattern):
    return pattern.astype(F32).astype(BF16)


def spread(pattern, rows, columns):
    across = dot_t(as_bf16(pattern), block_of(columns, pattern.shape[1])).astype(BF16)
    return dot(block_of(rows, pattern.shape[0]), across).astype(BF16)


def place(staged, values, index, count):
    half, tiles = values.shape[0] // 2, values.shape[1] // LANES
    for tile in range(tiles):
        columns = values[:, tile * LANES : (tile + 1) * LANES]
        staged[tile, pl.ds(index, half, stride=count), :] = columns[:half]
        staged[tiles + tile, pl.ds(index, half, stride=count), :] = columns[half:]


def finish(staged, out_ref):
    for tile in range(staged.shape[0]):
        out_ref[:, tile * LANES : (tile + 1) * LANES] = staged[tile].astype(BF16)


def rows_kernel(batch_ref, tensor_ref, mask_ref, out_ref, staged):
    count, rows, columns = tensor_ref.shape
    pattern = as_bf16(mask_ref[pl.ds(batch_ref[0], 1), :])
    keep = dot_t(pattern, block_of(columns, pattern.shape[1]))
    for index in range(count):
        place(staged, tensor_ref[index].astype(F32) * keep, index, count)
    finish(staged, out_ref)


def screened_kernel(
    batch_ref, tensor_ref, occ_ref, virt_ref, tmask_ref, omask_ref, vmask_ref, out_ref,
    keep, occ_part, virt_part, staged,
):
    index, count = pl.program_id(0), pl.num_programs(0)
    ao_count = virt_ref.shape[0]

    @pl.when(index == 0)
    def _():
        keep[...] = spread(tmask_ref[...], ao_count, ao_count)
        virt_part[...] = virt_ref[...] * spread(vmask_ref[...], ao_count, ao_count)
        pattern = as_bf16(omask_ref[pl.ds(batch_ref[0], 1), :])
        row_keep = dot_t(pattern, block_of(ao_count, pattern.shape[1])).astype(BF16)
        occ_part[...] = occ_ref[...] * row_keep

    half = dot(occ_part[...], tensor_ref[0] * keep[...]).astype(BF16)
    values = dot(half, virt_part[...])
    place(staged, values, index, 8)

    @pl.when(index == count - 1)
    def _():
        finish(staged, out_ref)


def row_messages(batch, tensor, tensor_mask, rows):
    count, _, columns = tensor.shape
    shape = (rows // 2 * count, 2 * columns)
    return pl.pallas_call(
        rows_kernel,
        out_shape=jax.ShapeDtypeStruct(shape, BF16),
        grid_spec=pltpu.PrefetchScalarGridSpec(
            num_scalar_prefetch=1,
            grid=(1,),
            in_specs=[
                pl.BlockSpec((count, rows, columns), lambda s, batch: (0, batch[0], 0)),
                pl.BlockSpec(tensor_mask.shape, lambda s, batch: (0, 0)),
            ],
            out_specs=pl.BlockSpec(shape, lambda s, batch: (0, 0)),
            scratch_shapes=[pltpu.VMEM((shape[1] // LANES, shape[0], LANES), F32)],
        ),
        compiler_params=pltpu.CompilerParams(vmem_limit_bytes=16 * 2**20),
        name="row_messages",
    )(batch, tensor, tensor_mask)


def screened_messages(batch, tensor, occ_green, virt_green, tensor_mask, occ_mask, virt_mask):
    count, ao_count, _ = tensor.shape
    rows = occ_green.shape[0]
    shape = (rows // 2 * count, 2 * ao_count)
    whole = lambda s, batch: (0, 0)
    pattern = pl.BlockSpec(tensor_mask.shape, whole)
    work = count * rows * ao_count * ao_count
    return pl.pallas_call(
        screened_kernel,
        out_shape=jax.ShapeDtypeStruct(shape, BF16),
        grid_spec=pltpu.PrefetchScalarGridSpec(
            num_scalar_prefetch=1,
            grid=(count,),
            in_specs=[
                pl.BlockSpec((1, ao_count, ao_count), lambda s, batch: (s, 0, 0)),
                pl.BlockSpec(occ_green.shape, whole),
                pl.BlockSpec(virt_green.shape, whole),
                pattern,
                pattern,
                pattern,
            ],
            out_specs=pl.BlockSpec(shape, whole),
            scratch_shapes=[
                pltpu.VMEM((ao_count, ao_count), BF16),
                pltpu.VMEM(occ_green.shape, BF16),
                pltpu.VMEM(virt_green.shape, BF16),
                pltpu.VMEM((shape[1] // LANES, shape[0], LANES), F32),
            ],
        ),
        compiler_params=pltpu.CompilerParams(vmem_limit_bytes=28 * 2**20),
        cost_estimate=pl.CostEstimate(
            flops=4 * work, bytes_accessed=2 * tensor.size + 4 * virt_green.size, transcendentals=0
        ),
        name="screened_messages",
    )(batch, tensor, occ_green, virt_green, tensor_mask, occ_mask, virt_mask)


def body(tensor, occ_green, virt_green, tensor_mask, occ_mask, virt_mask):
    rows_batch, ao_count = occ_green.shape
    local_ri = tensor.shape[0]
    batches = lax.axis_size("occ")
    cells = lax.axis_size("tens")
    chips = cells // 2
    same_core = [[2 * chip + core for chip in range(chips)] for core in range(2)]
    other_core = [(cell, cell ^ 1) for cell in range(cells)]
    batch = lax.axis_index("occ").astype(jnp.int32).reshape(1)
    core = lax.axis_index("tens") % 2

    def over_plane(values):
        return lax.all_to_all(values, "tens", 0, 0, axis_index_groups=same_core, tiled=True)

    def regroup(messages):
        moved = over_plane(messages.reshape(chips, local_ri, -1))
        return moved.reshape(chips * local_ri, -1)

    messages = row_messages(batch, tensor, tensor_mask, rows_batch)
    with jax.named_scope("rows"):
        moved_rows = regroup(messages)
    screened = screened_messages(
        batch, tensor, occ_green, virt_green, tensor_mask, occ_mask, virt_mask
    )
    moved_rows, screened = lax.optimization_barrier((moved_rows, screened))
    with jax.named_scope("other_rows"):
        sibling_rows = lax.ppermute(moved_rows, "tens", other_core)
    with jax.named_scope("screened"):
        moved_screened = regroup(screened)
    own = moved_rows.reshape(chips, 1, local_ri, -1)
    other = sibling_rows.reshape(chips, 1, local_ri, -1)
    first = jnp.where(core == 0, own, other)
    second = jnp.where(core == 0, other, own)
    all_rows = jnp.concatenate([first, second], axis=1).reshape(2 * chips * local_ri, -1)
    partial_value = dot_t(moved_screened, all_rows).astype(BF16)
    with jax.named_scope("over_plane"):
        shares = over_plane(partial_value.reshape(chips, local_ri, -1))
    batch_share = jnp.sum(shares.astype(F32), axis=0)
    copies = jnp.broadcast_to(batch_share[None], (batches,) + batch_share.shape)
    with jax.named_scope("over_batches"):
        batch_shares = lax.all_to_all(copies, "occ", 0, 0, tiled=True)
    return jnp.sum(batch_shares, axis=0) * (-1.0 / ao_count)


def solution(mesh):
    in_specs = (P("tens", None, None), P("occ", None), P(), P(), P(), P())
    out_specs = P("tens", None)
    return jax.shard_map(body, mesh=mesh, in_specs=in_specs, out_specs=out_specs, check_vma=False)
```

```python
import jax
import jax.numpy as jnp
from jax import lax
from jax.experimental import pallas as pl
from jax.experimental.pallas import tpu as pltpu
from jax.sharding import PartitionSpec as P

BLOCK = 64
LANES = 128
BF16 = jnp.bfloat16
F32 = jnp.float32


def block_of(size, blocks):
    position = lax.broadcasted_iota(jnp.int32, (size, blocks), 0)
    start = lax.broadcasted_iota(jnp.int32, (size, blocks), 1) * BLOCK
    return ((position >= start) & (position < start + BLOCK)).astype(BF16)


def dot(a, b):
    return jnp.dot(a, b, preferred_element_type=F32)


def dot_t(a, b):
    return lax.dot_general(a, b, (((1,), (1,)), ((), ())), preferred_element_type=F32)


def as_bf16(pattern):
    return pattern.astype(F32).astype(BF16)


def spread(pattern, rows, columns):
    across = dot_t(as_bf16(pattern), block_of(columns, pattern.shape[1])).astype(BF16)
    return dot(block_of(rows, pattern.shape[0]), across).astype(BF16)


def place(staged, values, index, count):
    half, tiles = values.shape[0] // 2, values.shape[1] // LANES
    for tile in range(tiles):
        columns = values[:, tile * LANES : (tile + 1) * LANES]
        staged[tile, pl.ds(index, half, stride=count), :] = columns[:half]
        staged[tiles + tile, pl.ds(index, half, stride=count), :] = columns[half:]


def finish(staged, out_ref):
    for tile in range(staged.shape[0]):
        out_ref[:, tile * LANES : (tile + 1) * LANES] = staged[tile].astype(BF16)


def rows_kernel(batch_ref, tensor_ref, mask_ref, out_ref, staged):
    count, rows, columns = tensor_ref.shape
    pattern = as_bf16(mask_ref[pl.ds(batch_ref[0], 1), :])
    keep = dot_t(pattern, block_of(columns, pattern.shape[1]))
    for index in range(count):
        place(staged, tensor_ref[index].astype(F32) * keep, index, count)
    finish(staged, out_ref)


def screened_kernel(
    batch_ref, tensor_ref, occ_ref, virt_ref, tmask_ref, omask_ref, vmask_ref, out_ref,
    keep, occ_part, virt_part, staged,
):
    index, count = pl.program_id(0), pl.num_programs(0)
    ao_count = virt_ref.shape[0]

    @pl.when(index == 0)
    def _():
        keep[...] = spread(tmask_ref[...], ao_count, ao_count)
        virt_part[...] = virt_ref[...] * spread(vmask_ref[...], ao_count, ao_count)
        pattern = as_bf16(omask_ref[pl.ds(batch_ref[0], 1), :])
        row_keep = dot_t(pattern, block_of(ao_count, pattern.shape[1])).astype(BF16)
        occ_part[...] = occ_ref[...] * row_keep

    half = dot(occ_part[...], tensor_ref[0] * keep[...]).astype(BF16)
    values = dot(half, virt_part[...])
    place(staged, values, index, 8)

    @pl.when(index == count - 1)
    def _():
        finish(staged, out_ref)


def row_messages(batch, tensor, tensor_mask, rows):
    count, _, columns = tensor.shape
    shape = (rows // 2 * count, 2 * columns)
    return pl.pallas_call(
        rows_kernel,
        out_shape=jax.ShapeDtypeStruct(shape, BF16),
        grid_spec=pltpu.PrefetchScalarGridSpec(
            num_scalar_prefetch=1,
            grid=(1,),
            in_specs=[
                pl.BlockSpec((count, rows, columns), lambda s, batch: (0, batch[0], 0)),
                pl.BlockSpec(tensor_mask.shape, lambda s, batch: (0, 0)),
            ],
            out_specs=pl.BlockSpec(shape, lambda s, batch: (0, 0)),
            scratch_shapes=[pltpu.VMEM((shape[1] // LANES, shape[0], LANES), F32)],
        ),
        compiler_params=pltpu.CompilerParams(vmem_limit_bytes=56 * 2**20),
        name="row_messages",
    )(batch, tensor, tensor_mask)


def screened_messages(batch, tensor, occ_green, virt_green, tensor_mask, occ_mask, virt_mask):
    count, ao_count, _ = tensor.shape
    rows = occ_green.shape[0]
    shape = (rows // 2 * count, 2 * ao_count)
    whole = lambda s, batch: (0, 0)
    pattern = pl.BlockSpec(tensor_mask.shape, whole)
    work = count * rows * ao_count * ao_count
    return pl.pallas_call(
        screened_kernel,
        out_shape=jax.ShapeDtypeStruct(shape, BF16),
        grid_spec=pltpu.PrefetchScalarGridSpec(
            num_scalar_prefetch=1,
            grid=(count,),
            in_specs=[
                pl.BlockSpec((1, ao_count, ao_count), lambda s, batch: (s, 0, 0)),
                pl.BlockSpec(occ_green.shape, whole),
                pl.BlockSpec(virt_green.shape, whole),
                pattern,
                pattern,
                pattern,
            ],
            out_specs=pl.BlockSpec(shape, whole),
            scratch_shapes=[
                pltpu.VMEM((ao_count, ao_count), BF16),
                pltpu.VMEM(occ_green.shape, BF16),
                pltpu.VMEM(virt_green.shape, BF16),
                pltpu.VMEM((shape[1] // LANES, shape[0], LANES), F32),
            ],
        ),
        compiler_params=pltpu.CompilerParams(vmem_limit_bytes=56 * 2**20),
        cost_estimate=pl.CostEstimate(
            flops=4 * work, bytes_accessed=2 * tensor.size + 4 * virt_green.size, transcendentals=0
        ),
        name="screened_messages",
    )(batch, tensor, occ_green, virt_green, tensor_mask, occ_mask, virt_mask)


def body(tensor, occ_green, virt_green, tensor_mask, occ_mask, virt_mask):
    rows_batch, ao_count = occ_green.shape
    local_ri = tensor.shape[0]
    batches = lax.axis_size("occ")
    cells = lax.axis_size("tens")
    chips = cells // 2
    same_core = [[2 * chip + core for chip in range(chips)] for core in range(2)]
    other_core = [(cell, cell ^ 1) for cell in range(cells)]
    batch = lax.axis_index("occ").astype(jnp.int32).reshape(1)
    core = lax.axis_index("tens") % 2

    def over_plane(values):
        return lax.all_to_all(values, "tens", 0, 0, axis_index_groups=same_core, tiled=True)

    def regroup(messages):
        moved = over_plane(messages.reshape(chips, local_ri, -1))
        return moved.reshape(chips * local_ri, -1)

    messages = row_messages(batch, tensor, tensor_mask, rows_batch)
    with jax.named_scope("rows"):
        moved_rows = regroup(messages)
    screened = screened_messages(
        batch, tensor, occ_green, virt_green, tensor_mask, occ_mask, virt_mask
    )
    moved_rows, screened = lax.optimization_barrier((moved_rows, screened))
    with jax.named_scope("other_rows"):
        sibling_rows = lax.ppermute(moved_rows, "tens", other_core)
    with jax.named_scope("screened"):
        moved_screened = regroup(screened)
    moved_screened, sibling_rows = lax.optimization_barrier((moved_screened, sibling_rows))
    own = moved_rows.reshape(chips, 1, local_ri, -1)
    other = sibling_rows.reshape(chips, 1, local_ri, -1)
    first = jnp.where(core == 0, own, other)
    second = jnp.where(core == 0, other, own)
    all_rows = jnp.concatenate([first, second], axis=1).reshape(2 * chips * local_ri, -1)
    partial_value = dot_t(moved_screened, all_rows).astype(BF16)
    with jax.named_scope("over_plane"):
        shares = over_plane(partial_value.reshape(chips, local_ri, -1))
    batch_share = jnp.sum(shares.astype(F32), axis=0)
    copies = jnp.broadcast_to(batch_share[None], (batches,) + batch_share.shape)
    with jax.named_scope("over_batches"):
        batch_shares = lax.all_to_all(copies, "occ", 0, 0, tiled=True)
    return jnp.sum(batch_shares, axis=0) * (-1.0 / ao_count)


def solution(mesh):
    in_specs = (P("tens", None, None), P("occ", None), P(), P(), P(), P())
    out_specs = P("tens", None)
    return jax.shard_map(body, mesh=mesh, in_specs=in_specs, out_specs=out_specs, check_vma=False)
```

```python
import functools

import jax
import jax.numpy as jnp
from jax import lax
from jax.experimental import pallas as pl
from jax.experimental.pallas import tpu as pltpu
from jax.sharding import PartitionSpec as P

BLOCK = 64
LANES = 128
BF16 = jnp.bfloat16
F32 = jnp.float32


def block_of(size, blocks):
    position = lax.broadcasted_iota(jnp.int32, (size, blocks), 0)
    start = lax.broadcasted_iota(jnp.int32, (size, blocks), 1) * BLOCK
    return ((position >= start) & (position < start + BLOCK)).astype(BF16)


def dot(a, b):
    return jnp.dot(a, b, preferred_element_type=F32)


def dot_t(a, b):
    return lax.dot_general(a, b, (((1,), (1,)), ((), ())), preferred_element_type=F32)


def as_bf16(pattern):
    return pattern.astype(F32).astype(BF16)


def spread(pattern, rows, columns):
    across = dot_t(as_bf16(pattern), block_of(columns, pattern.shape[1])).astype(BF16)
    return dot(block_of(rows, pattern.shape[0]), across).astype(BF16)


def kept_blocks(batch, mask_ref, kept):
    count = jnp.int32(0)
    for block in range(mask_ref.shape[1]):
        kept[count] = block
        count = count + mask_ref[batch, block]
    return count


def placement(rows, local_ri):
    shift = local_ri.bit_length() - 1
    to = lax.broadcasted_iota(jnp.int32, (rows, rows), 0)
    source = lax.broadcasted_iota(jnp.int32, (rows, rows), 1)
    wanted = (to & (local_ri - 1)) * (rows // local_ri) + (to >> shift)
    return (wanted == source).astype(F32).astype(BF16)


def gather_blocks(read, kept, count, out_ref, first, last):
    rows = out_ref.shape[0]
    side = lax.broadcasted_iota(jnp.int32, (rows, LANES), 1) // BLOCK
    for slot in range(first, last):
        columns = slice(slot * LANES, (slot + 1) * LANES)

        @pl.when(slot < count)
        def _():
            block = kept[slot]
            odd = block % 2
            direct = read(odd, block // 2)
            rolled = pltpu.roll(read(1 - odd, block // 2), BLOCK, 1)
            out_ref[:, columns] = jnp.where(side == odd, direct, rolled).astype(BF16)

        @pl.when(slot >= count)
        def _():
            out_ref[:, columns] = jnp.zeros((rows, LANES), BF16)


def rows_kernel(sizes, mask_hbm, tensor_ref, *refs):
    outs = refs[: len(sizes)]
    choice_hbm, mask_ref, choice_ref, slab, ordered, messages, kept, arrived = refs[len(sizes) :]
    local_ri, rows, columns = slab.shape
    chips = rows // 2
    batch = lax.axis_index("occ")
    start = pl.multiple_of(batch * rows, rows)
    mask_copy = pltpu.make_async_copy(mask_hbm, mask_ref, arrived.at[0])
    mask_copy.start()
    copy = pltpu.make_async_copy(tensor_ref.at[:, pl.ds(start, rows), :], slab, arrived.at[1])
    copy.start()
    place = placement(local_ri * chips, local_ri)
    mask_copy.wait()
    fullest = jnp.int32(0)
    for row in range(mask_ref.shape[0]):
        total = jnp.int32(0)
        for block in range(mask_ref.shape[1]):
            total = total + mask_ref[row, block]
        fullest = jnp.maximum(fullest, total)
    choice = jnp.clip(fullest - sizes[0], 0, len(sizes) - 1)
    choice_ref[0] = choice
    choice_copy = pltpu.make_async_copy(choice_ref, choice_hbm, arrived.at[2])
    choice_copy.start()
    count = kept_blocks(batch, mask_ref, kept)
    copy.wait()
    for half in range(2):
        values = slab[:, half * chips : (half + 1) * chips, :].reshape(local_ri * chips, columns)
        values = dot(place, values)
        for tile in range(columns // LANES):
            ordered[half, tile] = values[:, tile * LANES : (tile + 1) * LANES]

    def send(index, first, last, semaphore):
        columns = slice(first * LANES, last * LANES)
        return pltpu.make_async_copy(
            messages.at[:, columns], outs[index].at[:, columns], arrived.at[semaphore]
        )

    read = lambda half, tile: ordered[half, tile]
    gather_blocks(read, kept, count, messages, 0, sizes[0])
    for index in range(len(sizes)):

        @pl.when(choice == index)
        def _():
            send(index, 0, sizes[0], 3).start()

    gather_blocks(read, kept, count, messages, sizes[0], sizes[-1])
    for index, slots in enumerate(sizes):

        @pl.when(choice == index)
        def _():
            if slots > sizes[0]:
                rest = send(index, sizes[0], slots, 4)
                rest.start()
                rest.wait()
            send(index, 0, sizes[0], 3).wait()

    choice_copy.wait()


def screened_kernel(
    batch_ref, mask_ref, tensor_ref, occ_ref, virt_ref, tmask_ref, omask_ref, vmask_ref, out_ref,
    keep, occ_part, virt_part, occ_half, staged, kept,
):
    index = pl.program_id(0)
    local_ri = occ_half.shape[1]
    ao_count = virt_ref.shape[0]
    chips = occ_ref.shape[0] // 2

    @pl.when(index == 0)
    def _():
        keep[...] = spread(tmask_ref[...], ao_count, ao_count)
        virt_part[...] = virt_ref[...] * spread(vmask_ref[...], ao_count, ao_count)
        pattern = as_bf16(omask_ref[pl.ds(batch_ref[0], 1), :])
        row_keep = dot_t(pattern, block_of(ao_count, pattern.shape[1])).astype(BF16)
        occ_part[...] = occ_ref[...] * row_keep

    product = dot(occ_part[...], tensor_ref[0] * keep[...]).astype(BF16)
    occ_half[0, index] = product[:chips]
    occ_half[1, index] = product[chips:]

    @pl.when(index == local_ri - 1)
    def _():
        count = kept_blocks(batch_ref[0], mask_ref, kept)
        place = placement(local_ri * chips, local_ri)
        for half in range(2):
            values = dot(occ_half[half].reshape(local_ri * chips, ao_count), virt_part[...])
            ordered = dot(place, values.astype(BF16))
            for tile in range(ao_count // LANES):
                staged[half, tile] = ordered[:, tile * LANES : (tile + 1) * LANES]
        slots = out_ref.shape[1] // LANES
        gather_blocks(lambda half, tile: staged[half, tile], kept, count, out_ref, 0, slots)


def row_messages(sizes, tensor_mask, tensor, rows):
    local_ri, _, columns = tensor.shape
    count = rows // 2 * local_ri
    shapes = [jax.ShapeDtypeStruct((count, slots * LANES), BF16) for slots in sizes]
    anywhere = pl.BlockSpec(memory_space=pl.ANY)
    *messages, choice = pl.pallas_call(
        functools.partial(rows_kernel, sizes),
        out_shape=(*shapes, jax.ShapeDtypeStruct((1,), jnp.int32)),
        in_specs=[anywhere, anywhere],
        out_specs=(anywhere,) * (len(sizes) + 1),
        scratch_shapes=[
            pltpu.SMEM(tensor_mask.shape, jnp.int32),
            pltpu.SMEM((1,), jnp.int32),
            pltpu.VMEM((local_ri, rows, columns), BF16),
            pltpu.VMEM((2, columns // LANES, count, LANES), F32),
            pltpu.VMEM((count, 2 * columns), BF16),
            pltpu.SMEM((tensor_mask.shape[1] + 1,), jnp.int32),
            pltpu.SemaphoreType.DMA((5,)),
        ],
        compiler_params=pltpu.CompilerParams(vmem_limit_bytes=56 * 2**20),
        name="row_messages",
    )(tensor_mask, tensor)
    return messages, choice[0]


def screened_messages(
    slots, batch, tensor, occ_green, virt_green, tensor_mask, occ_mask, virt_mask
):
    local_ri, ao_count, _ = tensor.shape
    rows = occ_green.shape[0]
    chips = rows // 2
    whole = lambda s, batch, mask: (0, 0)
    pattern = pl.BlockSpec(tensor_mask.shape, whole)
    work = local_ri * rows * ao_count * ao_count
    return pl.pallas_call(
        screened_kernel,
        out_shape=jax.ShapeDtypeStruct((chips * local_ri, slots * LANES), BF16),
        grid_spec=pltpu.PrefetchScalarGridSpec(
            num_scalar_prefetch=2,
            grid=(local_ri,),
            in_specs=[
                pl.BlockSpec((1, ao_count, ao_count), lambda s, batch, mask: (s, 0, 0)),
                pl.BlockSpec(occ_green.shape, whole),
                pl.BlockSpec(virt_green.shape, whole),
                pattern,
                pattern,
                pattern,
            ],
            out_specs=pl.BlockSpec((chips * local_ri, slots * LANES), whole),
            scratch_shapes=[
                pltpu.VMEM((ao_count, ao_count), BF16),
                pltpu.VMEM(occ_green.shape, BF16),
                pltpu.VMEM(virt_green.shape, BF16),
                pltpu.VMEM((2, local_ri, chips, ao_count), BF16),
                pltpu.VMEM((2, ao_count // LANES, chips * local_ri, LANES), F32),
                pltpu.SMEM((tensor_mask.shape[1] + 1,), jnp.int32),
            ],
        ),
        compiler_params=pltpu.CompilerParams(vmem_limit_bytes=56 * 2**20),
        cost_estimate=pl.CostEstimate(
            flops=4 * work, bytes_accessed=2 * tensor.size + 4 * virt_green.size, transcendentals=0
        ),
        name="screened_messages",
    )(batch, tensor_mask, tensor, occ_green, virt_green, tensor_mask, occ_mask, virt_mask)


def body(tensor, occ_green, virt_green, tensor_mask, occ_mask, virt_mask):
    rows_batch, ao_count = occ_green.shape
    local_ri = tensor.shape[0]
    batches = lax.axis_size("occ")
    cells = lax.axis_size("tens")
    chips = cells // 2
    same_core = [[2 * chip + core for chip in range(chips)] for core in range(2)]
    other_core = [(cell, cell ^ 1) for cell in range(cells)]
    batch = lax.axis_index("occ").astype(jnp.int32).reshape(1)
    core = lax.axis_index("tens") % 2

    def over_plane(values):
        return lax.all_to_all(values, "tens", 0, 0, axis_index_groups=same_core, tiled=True)

    def regroup(messages):
        moved = over_plane(messages.reshape(chips, local_ri, -1))
        return moved.reshape(chips * local_ri, -1)

    blocks = tensor_mask.shape[1]
    sizes = list(range(blocks // 2, blocks + 1))
    messages, choice = row_messages(sizes, tensor_mask, tensor, rows_batch)

    def partial_with(index):
        slots = sizes[index]

        def partial_value():
            with jax.named_scope("rows"):
                moved_rows = regroup(messages[index])
            screened = screened_messages(
                slots, batch, tensor, occ_green, virt_green, tensor_mask, occ_mask, virt_mask
            )
            moved_rows, screened = lax.optimization_barrier((moved_rows, screened))
            with jax.named_scope("other_rows"):
                sibling_rows = lax.ppermute(moved_rows, "tens", other_core)
            with jax.named_scope("screened"):
                moved_screened = regroup(screened)
            moved_screened, sibling_rows = lax.optimization_barrier((moved_screened, sibling_rows))
            own = moved_rows.reshape(chips, 1, local_ri, -1)
            other = sibling_rows.reshape(chips, 1, local_ri, -1)
            first = jnp.where(core == 0, own, other)
            second = jnp.where(core == 0, other, own)
            all_rows = jnp.concatenate([first, second], axis=1)
            all_rows = all_rows.reshape(2 * chips * local_ri, -1)
            return dot_t(moved_screened, all_rows).astype(BF16)

        return partial_value

    branches = [partial_with(index) for index in range(len(sizes))]
    partial_value = lax.switch(choice, branches)
    with jax.named_scope("over_plane"):
        shares = over_plane(partial_value.reshape(chips, local_ri, -1))
    batch_share = jnp.sum(shares.astype(F32), axis=0)
    copies = jnp.broadcast_to(batch_share[None], (batches,) + batch_share.shape)
    with jax.named_scope("over_batches"):
        batch_shares = lax.all_to_all(copies, "occ", 0, 0, tiled=True)
    return jnp.sum(batch_shares, axis=0) * (-1.0 / ao_count)


def solution(mesh):
    in_specs = (P("tens", None, None), P("occ", None), P(), P(), P(), P())
    out_specs = P("tens", None)
    return jax.shard_map(body, mesh=mesh, in_specs=in_specs, out_specs=out_specs, check_vma=False)
```

```python
import functools

import jax
import jax.numpy as jnp
from jax import lax
from jax.experimental import pallas as pl
from jax.experimental.pallas import tpu as pltpu
from jax.sharding import PartitionSpec as P

BLOCK = 64
LANES = 128
BF16 = jnp.bfloat16
F32 = jnp.float32


def block_of(size, blocks):
    position = lax.broadcasted_iota(jnp.int32, (size, blocks), 0)
    start = lax.broadcasted_iota(jnp.int32, (size, blocks), 1) * BLOCK
    return ((position >= start) & (position < start + BLOCK)).astype(BF16)


def dot(a, b):
    return jnp.dot(a, b, preferred_element_type=F32)


def dot_t(a, b):
    return lax.dot_general(a, b, (((1,), (1,)), ((), ())), preferred_element_type=F32)


def as_bf16(pattern):
    return pattern.astype(F32).astype(BF16)


def spread(pattern, rows, columns):
    across = dot_t(as_bf16(pattern), block_of(columns, pattern.shape[1])).astype(BF16)
    return dot(block_of(rows, pattern.shape[0]), across).astype(BF16)


def kept_blocks(batch, mask_ref, kept):
    count = jnp.int32(0)
    for block in range(mask_ref.shape[1]):
        kept[count] = block
        count = count + mask_ref[batch, block]
    return count


def placement(rows, local_ri):
    shift = local_ri.bit_length() - 1
    to = lax.broadcasted_iota(jnp.int32, (rows, rows), 0)
    source = lax.broadcasted_iota(jnp.int32, (rows, rows), 1)
    wanted = (to & (local_ri - 1)) * (rows // local_ri) + (to >> shift)
    return (wanted == source).astype(F32).astype(BF16)


def gather_blocks(read, kept, count, out_ref, first, last):
    rows = out_ref.shape[0]
    side = lax.broadcasted_iota(jnp.int32, (rows, LANES), 1) // BLOCK
    for slot in range(first, last):
        columns = slice(slot * LANES, (slot + 1) * LANES)

        @pl.when(slot < count)
        def _():
            block = kept[slot]
            odd = block % 2
            direct = read(odd, block // 2)
            rolled = pltpu.roll(read(1 - odd, block // 2), BLOCK, 1)
            out_ref[:, columns] = jnp.where(side == odd, direct, rolled).astype(BF16)

        @pl.when(slot >= count)
        def _():
            out_ref[:, columns] = jnp.zeros((rows, LANES), BF16)


def rows_kernel(sizes, mask_hbm, tensor_ref, *refs):
    outs = refs[: len(sizes)]
    choice_hbm, mask_ref, choice_ref, slab, ordered, messages, kept, arrived = refs[len(sizes) :]
    local_ri, rows, columns = slab.shape
    chips = rows // 2
    batch = lax.axis_index("occ")
    start = pl.multiple_of(batch * rows, rows)
    mask_copy = pltpu.make_async_copy(mask_hbm, mask_ref, arrived.at[0])
    mask_copy.start()
    copy = pltpu.make_async_copy(tensor_ref.at[:, pl.ds(start, rows), :], slab, arrived.at[1])
    copy.start()
    place = placement(local_ri * chips, local_ri)
    mask_copy.wait()
    count = kept_blocks(batch, mask_ref, kept)
    choice = jnp.clip(count - sizes[0], 0, len(sizes) - 1)
    choice_ref[0] = choice
    choice_copy = pltpu.make_async_copy(choice_ref, choice_hbm, arrived.at[2])
    choice_copy.start()
    copy.wait()
    for half in range(2):
        values = slab[:, half * chips : (half + 1) * chips, :].reshape(local_ri * chips, columns)
        values = dot(place, values)
        for tile in range(columns // LANES):
            ordered[half, tile] = values[:, tile * LANES : (tile + 1) * LANES]

    def send(index, first, last, semaphore):
        columns = slice(first * LANES, last * LANES)
        return pltpu.make_async_copy(
            messages.at[:, columns], outs[index].at[:, columns], arrived.at[semaphore]
        )

    read = lambda half, tile: ordered[half, tile]
    gather_blocks(read, kept, count, messages, 0, sizes[0])
    for index in range(len(sizes)):

        @pl.when(choice == index)
        def _():
            send(index, 0, sizes[0], 3).start()

    gather_blocks(read, kept, count, messages, sizes[0], sizes[-1])
    for index, slots in enumerate(sizes):

        @pl.when(choice == index)
        def _():
            if slots > sizes[0]:
                rest = send(index, sizes[0], slots, 4)
                rest.start()
                rest.wait()
            send(index, 0, sizes[0], 3).wait()

    choice_copy.wait()


def screened_kernel(
    batch_ref, mask_ref, tensor_ref, occ_ref, virt_ref, tmask_ref, omask_ref, vmask_ref, out_ref,
    keep, occ_part, virt_part, occ_half, staged, kept,
):
    index = pl.program_id(0)
    local_ri = occ_half.shape[1]
    ao_count = virt_ref.shape[0]
    chips = occ_ref.shape[0] // 2

    @pl.when(index == 0)
    def _():
        keep[...] = spread(tmask_ref[...], ao_count, ao_count)
        virt_part[...] = virt_ref[...] * spread(vmask_ref[...], ao_count, ao_count)
        pattern = as_bf16(omask_ref[pl.ds(batch_ref[0], 1), :])
        row_keep = dot_t(pattern, block_of(ao_count, pattern.shape[1])).astype(BF16)
        occ_part[...] = occ_ref[...] * row_keep

    product = dot(occ_part[...], tensor_ref[0] * keep[...]).astype(BF16)
    occ_half[0, index] = product[:chips]
    occ_half[1, index] = product[chips:]

    @pl.when(index == local_ri - 1)
    def _():
        count = kept_blocks(batch_ref[0], mask_ref, kept)
        place = placement(local_ri * chips, local_ri)
        for half in range(2):
            values = dot(occ_half[half].reshape(local_ri * chips, ao_count), virt_part[...])
            ordered = dot(place, values.astype(BF16))
            for tile in range(ao_count // LANES):
                staged[half, tile] = ordered[:, tile * LANES : (tile + 1) * LANES]
        slots = out_ref.shape[1] // LANES
        gather_blocks(lambda half, tile: staged[half, tile], kept, count, out_ref, 0, slots)


def row_messages(sizes, tensor_mask, tensor, rows):
    local_ri, _, columns = tensor.shape
    count = rows // 2 * local_ri
    shapes = [jax.ShapeDtypeStruct((count, slots * LANES), BF16) for slots in sizes]
    anywhere = pl.BlockSpec(memory_space=pl.ANY)
    *messages, choice = pl.pallas_call(
        functools.partial(rows_kernel, sizes),
        out_shape=(*shapes, jax.ShapeDtypeStruct((1,), jnp.int32)),
        in_specs=[anywhere, anywhere],
        out_specs=(anywhere,) * (len(sizes) + 1),
        scratch_shapes=[
            pltpu.SMEM(tensor_mask.shape, jnp.int32),
            pltpu.SMEM((1,), jnp.int32),
            pltpu.VMEM((local_ri, rows, columns), BF16),
            pltpu.VMEM((2, columns // LANES, count, LANES), F32),
            pltpu.VMEM((count, 2 * columns), BF16),
            pltpu.SMEM((tensor_mask.shape[1] + 1,), jnp.int32),
            pltpu.SemaphoreType.DMA((5,)),
        ],
        compiler_params=pltpu.CompilerParams(vmem_limit_bytes=56 * 2**20),
        name="row_messages",
    )(tensor_mask, tensor)
    return messages, choice[0]


def screened_messages(
    slots, batch, tensor, occ_green, virt_green, tensor_mask, occ_mask, virt_mask
):
    local_ri, ao_count, _ = tensor.shape
    rows = occ_green.shape[0]
    chips = rows // 2
    whole = lambda s, batch, mask: (0, 0)
    pattern = pl.BlockSpec(tensor_mask.shape, whole)
    work = local_ri * rows * ao_count * ao_count
    return pl.pallas_call(
        screened_kernel,
        out_shape=jax.ShapeDtypeStruct((chips * local_ri, slots * LANES), BF16),
        grid_spec=pltpu.PrefetchScalarGridSpec(
            num_scalar_prefetch=2,
            grid=(local_ri,),
            in_specs=[
                pl.BlockSpec((1, ao_count, ao_count), lambda s, batch, mask: (s, 0, 0)),
                pl.BlockSpec(occ_green.shape, whole),
                pl.BlockSpec(virt_green.shape, whole),
                pattern,
                pattern,
                pattern,
            ],
            out_specs=pl.BlockSpec((chips * local_ri, slots * LANES), whole),
            scratch_shapes=[
                pltpu.VMEM((ao_count, ao_count), BF16),
                pltpu.VMEM(occ_green.shape, BF16),
                pltpu.VMEM(virt_green.shape, BF16),
                pltpu.VMEM((2, local_ri, chips, ao_count), BF16),
                pltpu.VMEM((2, ao_count // LANES, chips * local_ri, LANES), F32),
                pltpu.SMEM((tensor_mask.shape[1] + 1,), jnp.int32),
            ],
        ),
        compiler_params=pltpu.CompilerParams(vmem_limit_bytes=56 * 2**20),
        cost_estimate=pl.CostEstimate(
            flops=4 * work, bytes_accessed=2 * tensor.size + 4 * virt_green.size, transcendentals=0
        ),
        name="screened_messages",
    )(batch, tensor_mask, tensor, occ_green, virt_green, tensor_mask, occ_mask, virt_mask)


def body(tensor, occ_green, virt_green, tensor_mask, occ_mask, virt_mask):
    rows_batch, ao_count = occ_green.shape
    local_ri = tensor.shape[0]
    batches = lax.axis_size("occ")
    cells = lax.axis_size("tens")
    chips = cells // 2
    same_core = [[2 * chip + core for chip in range(chips)] for core in range(2)]
    other_core = [(cell, cell ^ 1) for cell in range(cells)]
    batch = lax.axis_index("occ").astype(jnp.int32).reshape(1)
    core = lax.axis_index("tens") % 2

    def over_plane(values):
        return lax.all_to_all(values, "tens", 0, 0, axis_index_groups=same_core, tiled=True)

    def regroup(messages):
        moved = over_plane(messages.reshape(chips, local_ri, -1))
        return moved.reshape(chips * local_ri, -1)

    blocks = tensor_mask.shape[1]
    sizes = list(range(blocks // 2, blocks + 1))
    messages, choice = row_messages(sizes, tensor_mask, tensor, rows_batch)

    def partial_with(index):
        slots = sizes[index]

        def partial_value():
            with jax.named_scope("rows"):
                moved_rows = regroup(messages[index])
            screened = screened_messages(
                slots, batch, tensor, occ_green, virt_green, tensor_mask, occ_mask, virt_mask
            )
            moved_rows, screened = lax.optimization_barrier((moved_rows, screened))
            with jax.named_scope("other_rows"):
                sibling_rows = lax.ppermute(moved_rows, "tens", other_core)
            with jax.named_scope("screened"):
                moved_screened = regroup(screened)
            moved_screened, sibling_rows = lax.optimization_barrier((moved_screened, sibling_rows))
            own = moved_rows.reshape(chips, 1, local_ri, -1)
            other = sibling_rows.reshape(chips, 1, local_ri, -1)
            first = jnp.where(core == 0, own, other)
            second = jnp.where(core == 0, other, own)
            all_rows = jnp.concatenate([first, second], axis=1)
            all_rows = all_rows.reshape(2 * chips * local_ri, -1)
            return dot_t(moved_screened, all_rows).astype(BF16)

        return partial_value

    branches = [partial_with(index) for index in range(len(sizes))]
    partial_value = lax.switch(choice, branches)
    with jax.named_scope("over_plane"):
        shares = over_plane(partial_value.reshape(chips, local_ri, -1))
    batch_share = jnp.sum(shares.astype(F32), axis=0)
    copies = jnp.broadcast_to(batch_share[None], (batches,) + batch_share.shape)
    with jax.named_scope("over_batches"):
        batch_shares = lax.all_to_all(copies, "occ", 0, 0, tiled=True)
    return jnp.sum(batch_shares, axis=0) * (-1.0 / ao_count)


def solution(mesh):
    in_specs = (P("tens", None, None), P("occ", None), P(), P(), P(), P())
    out_specs = P("tens", None)
    return jax.shard_map(body, mesh=mesh, in_specs=in_specs, out_specs=out_specs, check_vma=False)
```

```python
import functools

import jax
import jax.numpy as jnp
from jax import lax
from jax.experimental import pallas as pl
from jax.experimental.pallas import tpu as pltpu
from jax.sharding import PartitionSpec as P

BLOCK = 64
LANES = 128
BF16 = jnp.bfloat16
F32 = jnp.float32


def block_of(size, blocks):
    position = lax.broadcasted_iota(jnp.int32, (size, blocks), 0)
    start = lax.broadcasted_iota(jnp.int32, (size, blocks), 1) * BLOCK
    return ((position >= start) & (position < start + BLOCK)).astype(BF16)


def dot(a, b):
    return jnp.dot(a, b, preferred_element_type=F32)


def dot_t(a, b):
    return lax.dot_general(a, b, (((1,), (1,)), ((), ())), preferred_element_type=F32)


def as_bf16(pattern):
    return pattern.astype(F32).astype(BF16)


def spread(pattern, rows, columns):
    across = dot_t(as_bf16(pattern), block_of(columns, pattern.shape[1])).astype(BF16)
    return dot(block_of(rows, pattern.shape[0]), across).astype(BF16)


def kept_blocks(batch, mask_ref, kept):
    count = jnp.int32(0)
    for block in range(mask_ref.shape[1]):
        kept[count] = block
        count = count + mask_ref[batch, block]
    return count


def placement(rows, local_ri):
    shift = local_ri.bit_length() - 1
    to = lax.broadcasted_iota(jnp.int32, (rows, rows), 0)
    source = lax.broadcasted_iota(jnp.int32, (rows, rows), 1)
    wanted = (to & (local_ri - 1)) * (rows // local_ri) + (to >> shift)
    return (wanted == source).astype(F32).astype(BF16)


def gather_blocks(read, kept, count, out_ref, first, last):
    rows = out_ref.shape[0]
    side = lax.broadcasted_iota(jnp.int32, (rows, LANES), 1) // BLOCK
    for slot in range(first, last):
        columns = slice(slot * LANES, (slot + 1) * LANES)

        @pl.when(slot < count)
        def _():
            block = kept[slot]
            odd = block % 2
            direct = read(odd, block // 2)
            rolled = pltpu.roll(read(1 - odd, block // 2), BLOCK, 1)
            out_ref[:, columns] = jnp.where(side == odd, direct, rolled).astype(BF16)

        @pl.when(slot >= count)
        def _():
            out_ref[:, columns] = jnp.zeros((rows, LANES), BF16)


def rows_kernel(sizes, mask_hbm, tensor_ref, *refs):
    outs = refs[: len(sizes)]
    choice_hbm, mask_ref, choice_ref, slab, ordered, messages, kept, arrived = refs[len(sizes) :]
    local_ri, rows, columns = slab.shape
    chips = rows // 2
    batch = lax.axis_index("occ")
    start = pl.multiple_of(batch * rows, rows)
    mask_copy = pltpu.make_async_copy(mask_hbm, mask_ref, arrived.at[0])
    mask_copy.start()
    copy = pltpu.make_async_copy(tensor_ref.at[:, pl.ds(start, rows), :], slab, arrived.at[1])
    copy.start()
    place = placement(local_ri * chips, local_ri)
    mask_copy.wait()
    count = kept_blocks(batch, mask_ref, kept)
    choice = jnp.clip(count - sizes[0], 0, len(sizes) - 1)
    choice_ref[0] = choice
    choice_copy = pltpu.make_async_copy(choice_ref, choice_hbm, arrived.at[2])
    choice_copy.start()
    copy.wait()
    for half in range(2):
        values = slab[:, half * chips : (half + 1) * chips, :].reshape(local_ri * chips, columns)
        values = dot(place, values)
        for tile in range(columns // LANES):
            ordered[half, tile] = values[:, tile * LANES : (tile + 1) * LANES]

    def send(index, first, last, semaphore):
        columns = slice(first * LANES, last * LANES)
        return pltpu.make_async_copy(
            messages.at[:, columns], outs[index].at[:, columns], arrived.at[semaphore]
        )

    read = lambda half, tile: ordered[half, tile]
    gather_blocks(read, kept, count, messages, 0, sizes[0])
    for index in range(len(sizes)):

        @pl.when(choice == index)
        def _():
            send(index, 0, sizes[0], 3).start()

    gather_blocks(read, kept, count, messages, sizes[0], sizes[-1])
    for index, slots in enumerate(sizes):

        @pl.when(choice == index)
        def _():
            if slots > sizes[0]:
                rest = send(index, sizes[0], slots, 4)
                rest.start()
                rest.wait()
            send(index, 0, sizes[0], 3).wait()

    choice_copy.wait()


def screened_kernel(
    batch_ref, mask_ref, tensor_ref, occ_ref, virt_ref, tmask_ref, omask_ref, vmask_ref, out_ref,
    loaded, keep, occ_part, virt_part, occ_half, staged, kept, arrived,
):
    local_ri = occ_half.shape[1]
    ao_count = virt_ref.shape[0]
    chips = occ_ref.shape[0] // 2

    def copy(index):
        return pltpu.make_async_copy(
            tensor_ref.at[index], loaded.at[index], arrived.at[index]
        )

    for index in range(local_ri):
        copy(index).start()
    keep[...] = spread(tmask_ref[...], ao_count, ao_count)
    pattern = as_bf16(omask_ref[pl.ds(batch_ref[0], 1), :])
    row_keep = dot_t(pattern, block_of(ao_count, pattern.shape[1])).astype(BF16)
    occ_part[...] = occ_ref[...] * row_keep
    virt_part[...] = virt_ref[...] * spread(vmask_ref[...], ao_count, ao_count)

    def step(index, carry):
        copy(index).wait()
        product = dot(occ_part[...], loaded[index] * keep[...]).astype(BF16)
        occ_half[0, index] = product[:chips]
        occ_half[1, index] = product[chips:]
        return carry

    lax.fori_loop(0, local_ri, step, 0)
    count = kept_blocks(batch_ref[0], mask_ref, kept)
    place = placement(local_ri * chips, local_ri)
    for half in range(2):
        values = dot(occ_half[half].reshape(local_ri * chips, ao_count), virt_part[...])
        ordered = dot(place, values.astype(BF16))
        for tile in range(ao_count // LANES):
            staged[half, tile] = ordered[:, tile * LANES : (tile + 1) * LANES]
    slots = out_ref.shape[1] // LANES
    gather_blocks(lambda half, tile: staged[half, tile], kept, count, out_ref, 0, slots)


def row_messages(sizes, tensor_mask, tensor, rows):
    local_ri, _, columns = tensor.shape
    count = rows // 2 * local_ri
    shapes = [jax.ShapeDtypeStruct((count, slots * LANES), BF16) for slots in sizes]
    anywhere = pl.BlockSpec(memory_space=pl.ANY)
    *messages, choice = pl.pallas_call(
        functools.partial(rows_kernel, sizes),
        out_shape=(*shapes, jax.ShapeDtypeStruct((1,), jnp.int32)),
        in_specs=[anywhere, anywhere],
        out_specs=(anywhere,) * (len(sizes) + 1),
        scratch_shapes=[
            pltpu.SMEM(tensor_mask.shape, jnp.int32),
            pltpu.SMEM((1,), jnp.int32),
            pltpu.VMEM((local_ri, rows, columns), BF16),
            pltpu.VMEM((2, columns // LANES, count, LANES), F32),
            pltpu.VMEM((count, 2 * columns), BF16),
            pltpu.SMEM((tensor_mask.shape[1] + 1,), jnp.int32),
            pltpu.SemaphoreType.DMA((5,)),
        ],
        compiler_params=pltpu.CompilerParams(vmem_limit_bytes=56 * 2**20),
        name="row_messages",
    )(tensor_mask, tensor)
    return messages, choice[0]


def screened_messages(
    slots, batch, tensor, occ_green, virt_green, tensor_mask, occ_mask, virt_mask
):
    local_ri, ao_count, _ = tensor.shape
    rows = occ_green.shape[0]
    chips = rows // 2
    local = pl.BlockSpec(memory_space=pltpu.VMEM)
    work = local_ri * rows * ao_count * ao_count
    return pl.pallas_call(
        screened_kernel,
        out_shape=jax.ShapeDtypeStruct((chips * local_ri, slots * LANES), BF16),
        grid_spec=pltpu.PrefetchScalarGridSpec(
            num_scalar_prefetch=2,
            grid=(),
            in_specs=[pl.BlockSpec(memory_space=pl.ANY)] + [local] * 5,
            out_specs=local,
            scratch_shapes=[
                pltpu.VMEM(tensor.shape, BF16),
                pltpu.VMEM((ao_count, ao_count), BF16),
                pltpu.VMEM(occ_green.shape, BF16),
                pltpu.VMEM(virt_green.shape, BF16),
                pltpu.VMEM((2, local_ri, chips, ao_count), BF16),
                pltpu.VMEM((2, ao_count // LANES, chips * local_ri, LANES), F32),
                pltpu.SMEM((tensor_mask.shape[1] + 1,), jnp.int32),
                pltpu.SemaphoreType.DMA((local_ri,)),
            ],
        ),
        compiler_params=pltpu.CompilerParams(vmem_limit_bytes=56 * 2**20),
        cost_estimate=pl.CostEstimate(
            flops=4 * work, bytes_accessed=2 * tensor.size + 4 * virt_green.size, transcendentals=0
        ),
        name="screened_messages",
    )(batch, tensor_mask, tensor, occ_green, virt_green, tensor_mask, occ_mask, virt_mask)


def body(tensor, occ_green, virt_green, tensor_mask, occ_mask, virt_mask):
    rows_batch, ao_count = occ_green.shape
    local_ri = tensor.shape[0]
    batches = lax.axis_size("occ")
    cells = lax.axis_size("tens")
    chips = cells // 2
    same_core = [[2 * chip + core for chip in range(chips)] for core in range(2)]
    other_core = [(cell, cell ^ 1) for cell in range(cells)]
    batch = lax.axis_index("occ").astype(jnp.int32).reshape(1)
    core = lax.axis_index("tens") % 2

    def over_plane(values):
        return lax.all_to_all(values, "tens", 0, 0, axis_index_groups=same_core, tiled=True)

    def regroup(messages):
        moved = over_plane(messages.reshape(chips, local_ri, -1))
        return moved.reshape(chips * local_ri, -1)

    blocks = tensor_mask.shape[1]
    sizes = list(range(blocks // 2, blocks + 1))
    messages, choice = row_messages(sizes, tensor_mask, tensor, rows_batch)

    def partial_with(index):
        slots = sizes[index]

        def partial_value():
            with jax.named_scope("rows"):
                moved_rows = regroup(messages[index])
            screened = screened_messages(
                slots, batch, tensor, occ_green, virt_green, tensor_mask, occ_mask, virt_mask
            )
            moved_rows, screened = lax.optimization_barrier((moved_rows, screened))
            with jax.named_scope("other_rows"):
                sibling_rows = lax.ppermute(moved_rows, "tens", other_core)
            with jax.named_scope("screened"):
                moved_screened = regroup(screened)
            moved_screened, sibling_rows = lax.optimization_barrier((moved_screened, sibling_rows))
            own = moved_rows.reshape(chips, 1, local_ri, -1)
            other = sibling_rows.reshape(chips, 1, local_ri, -1)
            first = jnp.where(core == 0, own, other)
            second = jnp.where(core == 0, other, own)
            all_rows = jnp.concatenate([first, second], axis=1)
            all_rows = all_rows.reshape(2 * chips * local_ri, -1)
            return dot_t(moved_screened, all_rows).astype(BF16)

        return partial_value

    branches = [partial_with(index) for index in range(len(sizes))]
    partial_value = lax.switch(choice, branches)
    with jax.named_scope("over_plane"):
        shares = over_plane(partial_value.reshape(chips, local_ri, -1))
    batch_share = jnp.sum(shares.astype(F32), axis=0)
    copies = jnp.broadcast_to(batch_share[None], (batches,) + batch_share.shape)
    with jax.named_scope("over_batches"):
        batch_shares = lax.all_to_all(copies, "occ", 0, 0, tiled=True)
    return jnp.sum(batch_shares, axis=0) * (-1.0 / ao_count)


def solution(mesh):
    in_specs = (P("tens", None, None), P("occ", None), P(), P(), P(), P())
    out_specs = P("tens", None)
    return jax.shard_map(body, mesh=mesh, in_specs=in_specs, out_specs=out_specs, check_vma=False)
```

```python
import functools

import jax
import jax.numpy as jnp
from jax import lax
from jax.experimental import pallas as pl
from jax.experimental.pallas import tpu as pltpu
from jax.sharding import PartitionSpec as P

BLOCK = 64
LANES = 128
BF16 = jnp.bfloat16
F32 = jnp.float32


def block_of(size, blocks):
    position = lax.broadcasted_iota(jnp.int32, (size, blocks), 0)
    start = lax.broadcasted_iota(jnp.int32, (size, blocks), 1) * BLOCK
    return ((position >= start) & (position < start + BLOCK)).astype(BF16)


def dot(a, b):
    return jnp.dot(a, b, preferred_element_type=F32)


def dot_t(a, b):
    return lax.dot_general(a, b, (((1,), (1,)), ((), ())), preferred_element_type=F32)


def as_bf16(pattern):
    return pattern.astype(F32).astype(BF16)


def spread(pattern, rows, columns):
    across = dot_t(as_bf16(pattern), block_of(columns, pattern.shape[1])).astype(BF16)
    return dot(block_of(rows, pattern.shape[0]), across).astype(BF16)


def kept_blocks(batch, mask_ref, kept):
    count = jnp.int32(0)
    for block in range(mask_ref.shape[1]):
        kept[count] = block
        count = count + mask_ref[batch, block]
    return count


def placement(rows, local_ri):
    shift = local_ri.bit_length() - 1
    to = lax.broadcasted_iota(jnp.int32, (rows, rows), 0)
    source = lax.broadcasted_iota(jnp.int32, (rows, rows), 1)
    wanted = (to & (local_ri - 1)) * (rows // local_ri) + (to >> shift)
    return (wanted == source).astype(F32).astype(BF16)


def gather_blocks(read, kept, count, out_ref, first, last):
    rows = out_ref.shape[0]
    side = lax.broadcasted_iota(jnp.int32, (rows, LANES), 1) // BLOCK
    for slot in range(first, last):
        columns = slice(slot * LANES, (slot + 1) * LANES)

        @pl.when(slot < count)
        def _():
            block = kept[slot]
            odd = block % 2
            direct = read(odd, block // 2)
            rolled = pltpu.roll(read(1 - odd, block // 2), BLOCK, 1)
            out_ref[:, columns] = jnp.where(side == odd, direct, rolled).astype(BF16)

        @pl.when(slot >= count)
        def _():
            out_ref[:, columns] = jnp.zeros((rows, LANES), BF16)


def rows_kernel(sizes, mask_hbm, tensor_ref, *refs):
    outs = refs[: len(sizes)]
    choice_hbm, mask_ref, choice_ref, slab, ordered, messages, kept, arrived = refs[len(sizes) :]
    local_ri, rows, columns = slab.shape
    chips = rows // 2
    batch = lax.axis_index("occ")
    start = pl.multiple_of(batch * rows, rows)
    mask_copy = pltpu.make_async_copy(mask_hbm, mask_ref, arrived.at[0])
    mask_copy.start()
    copy = pltpu.make_async_copy(tensor_ref.at[:, pl.ds(start, rows), :], slab, arrived.at[1])
    copy.start()
    place = placement(local_ri * chips, local_ri)
    mask_copy.wait()
    count = kept_blocks(batch, mask_ref, kept)
    choice = jnp.clip(count - sizes[0], 0, len(sizes) - 1)
    choice_ref[0] = choice
    choice_copy = pltpu.make_async_copy(choice_ref, choice_hbm, arrived.at[2])
    choice_copy.start()
    copy.wait()
    for half in range(2):
        values = slab[:, half * chips : (half + 1) * chips, :].reshape(local_ri * chips, columns)
        values = dot(place, values)
        for tile in range(columns // LANES):
            ordered[half, tile] = values[:, tile * LANES : (tile + 1) * LANES]

    def send(index, first, last, semaphore):
        columns = slice(first * LANES, last * LANES)
        return pltpu.make_async_copy(
            messages.at[:, columns], outs[index].at[:, columns], arrived.at[semaphore]
        )

    read = lambda half, tile: ordered[half, tile]
    gather_blocks(read, kept, count, messages, 0, sizes[0])
    for index in range(len(sizes)):

        @pl.when(choice == index)
        def _():
            send(index, 0, sizes[0], 3).start()

    gather_blocks(read, kept, count, messages, sizes[0], sizes[-1])
    for index, slots in enumerate(sizes):

        @pl.when(choice == index)
        def _():
            if slots > sizes[0]:
                rest = send(index, sizes[0], slots, 4)
                rest.start()
                rest.wait()
            send(index, 0, sizes[0], 3).wait()

    choice_copy.wait()


def screened_kernel(
    batch_ref, mask_ref, tensor_ref, occ_ref, virt_ref, tmask_ref, omask_ref, vmask_ref, out_ref,
    loaded, keep, occ_part, virt_part, occ_half, staged, kept, arrived,
):
    local_ri = occ_half.shape[1]
    ao_count = virt_ref.shape[0]
    chips = occ_ref.shape[0] // 2

    def copy(index):
        return pltpu.make_async_copy(
            tensor_ref.at[index], loaded.at[index], arrived.at[index]
        )

    for index in range(local_ri):
        copy(index).start()
    keep[...] = spread(tmask_ref[...], ao_count, ao_count)
    pattern = as_bf16(omask_ref[pl.ds(batch_ref[0], 1), :])
    row_keep = dot_t(pattern, block_of(ao_count, pattern.shape[1])).astype(BF16)
    occ_part[...] = occ_ref[...] * row_keep
    virt_part[...] = virt_ref[...] * spread(vmask_ref[...], ao_count, ao_count)

    def step(index, carry):
        copy(index).wait()
        product = dot(occ_part[...], loaded[index] * keep[...]).astype(BF16)
        occ_half[0, index] = product[:chips]
        occ_half[1, index] = product[chips:]
        return carry

    lax.fori_loop(0, local_ri, step, 0)
    count = kept_blocks(batch_ref[0], mask_ref, kept)
    place = placement(local_ri * chips, local_ri)
    for half in range(2):
        values = dot(occ_half[half].reshape(local_ri * chips, ao_count), virt_part[...])
        ordered = dot(place, values.astype(BF16))
        for tile in range(ao_count // LANES):
            staged[half, tile] = ordered[:, tile * LANES : (tile + 1) * LANES]
    slots = out_ref.shape[1] // LANES
    gather_blocks(lambda half, tile: staged[half, tile], kept, count, out_ref, 0, slots)


def row_messages(sizes, tensor_mask, tensor, rows):
    local_ri, _, columns = tensor.shape
    count = rows // 2 * local_ri
    shapes = [jax.ShapeDtypeStruct((count, slots * LANES), BF16) for slots in sizes]
    anywhere = pl.BlockSpec(memory_space=pl.ANY)
    *messages, choice = pl.pallas_call(
        functools.partial(rows_kernel, sizes),
        out_shape=(*shapes, jax.ShapeDtypeStruct((1,), jnp.int32)),
        in_specs=[anywhere, anywhere],
        out_specs=(anywhere,) * (len(sizes) + 1),
        scratch_shapes=[
            pltpu.SMEM(tensor_mask.shape, jnp.int32),
            pltpu.SMEM((1,), jnp.int32),
            pltpu.VMEM((local_ri, rows, columns), BF16),
            pltpu.VMEM((2, columns // LANES, count, LANES), F32),
            pltpu.VMEM((count, 2 * columns), BF16),
            pltpu.SMEM((tensor_mask.shape[1] + 1,), jnp.int32),
            pltpu.SemaphoreType.DMA((5,)),
        ],
        compiler_params=pltpu.CompilerParams(vmem_limit_bytes=56 * 2**20),
        name="row_messages",
    )(tensor_mask, tensor)
    return messages, choice[0]


def screened_messages(
    slots, batch, tensor, occ_green, virt_green, tensor_mask, occ_mask, virt_mask
):
    local_ri, ao_count, _ = tensor.shape
    rows = occ_green.shape[0]
    chips = rows // 2
    local = pl.BlockSpec(memory_space=pltpu.VMEM)
    work = local_ri * rows * ao_count * ao_count
    return pl.pallas_call(
        screened_kernel,
        out_shape=jax.ShapeDtypeStruct((chips * local_ri, slots * LANES), BF16),
        grid_spec=pltpu.PrefetchScalarGridSpec(
            num_scalar_prefetch=2,
            grid=(),
            in_specs=[pl.BlockSpec(memory_space=pl.ANY)] + [local] * 5,
            out_specs=local,
            scratch_shapes=[
                pltpu.VMEM(tensor.shape, BF16),
                pltpu.VMEM((ao_count, ao_count), BF16),
                pltpu.VMEM(occ_green.shape, BF16),
                pltpu.VMEM(virt_green.shape, BF16),
                pltpu.VMEM((2, local_ri, chips, ao_count), BF16),
                pltpu.VMEM((2, ao_count // LANES, chips * local_ri, LANES), F32),
                pltpu.SMEM((tensor_mask.shape[1] + 1,), jnp.int32),
                pltpu.SemaphoreType.DMA((local_ri,)),
            ],
        ),
        compiler_params=pltpu.CompilerParams(vmem_limit_bytes=56 * 2**20),
        cost_estimate=pl.CostEstimate(
            flops=4 * work, bytes_accessed=2 * tensor.size + 4 * virt_green.size, transcendentals=0
        ),
        name="screened_messages",
    )(batch, tensor_mask, tensor, occ_green, virt_green, tensor_mask, occ_mask, virt_mask)


def body(tensor, occ_green, virt_green, tensor_mask, occ_mask, virt_mask):
    rows_batch, ao_count = occ_green.shape
    local_ri = tensor.shape[0]
    batches = lax.axis_size("occ")
    cells = lax.axis_size("tens")
    chips = cells // 2
    same_core = [[2 * chip + core for chip in range(chips)] for core in range(2)]
    other_core = [(cell, cell ^ 1) for cell in range(cells)]
    batch = lax.axis_index("occ").astype(jnp.int32).reshape(1)
    core = lax.axis_index("tens") % 2

    def over_plane(values):
        return lax.all_to_all(values, "tens", 0, 0, axis_index_groups=same_core, tiled=True)

    def regroup(messages):
        moved = over_plane(messages.reshape(chips, local_ri, -1))
        return moved.reshape(chips * local_ri, -1)

    blocks = tensor_mask.shape[1]
    sizes = list(range(blocks // 2, blocks + 1))
    messages, choice = row_messages(sizes, tensor_mask, tensor, rows_batch)

    def partial_with(index):
        slots = sizes[index]

        def partial_value():
            with jax.named_scope("rows"):
                moved_rows = regroup(messages[index])
            screened = screened_messages(
                slots, batch, tensor, occ_green, virt_green, tensor_mask, occ_mask, virt_mask
            )
            moved_rows, screened = lax.optimization_barrier((moved_rows, screened))
            with jax.named_scope("other_rows"):
                sibling_rows = lax.ppermute(moved_rows, "tens", other_core)
            with jax.named_scope("screened"):
                moved_screened = regroup(screened)
            moved_screened, sibling_rows = lax.optimization_barrier((moved_screened, sibling_rows))
            own = moved_rows.reshape(chips, 1, local_ri, -1)
            other = sibling_rows.reshape(chips, 1, local_ri, -1)
            first = jnp.where(core == 0, own, other)
            second = jnp.where(core == 0, other, own)
            all_rows = jnp.concatenate([first, second], axis=1)
            all_rows = all_rows.reshape(2 * chips * local_ri, -1)
            return dot_t(moved_screened, all_rows).astype(BF16)

        return partial_value

    branches = [partial_with(index) for index in range(len(sizes))]
    partial_value = lax.switch(choice, branches)
    with jax.named_scope("over_plane"):
        shares = over_plane(partial_value.reshape(chips, local_ri, -1))
    batch_share = jnp.sum(shares.astype(F32), axis=0)
    copies = jnp.broadcast_to(batch_share.astype(BF16)[None], (batches,) + batch_share.shape)
    with jax.named_scope("over_batches"):
        batch_shares = lax.all_to_all(copies, "occ", 0, 0, tiled=True)
    return jnp.sum(batch_shares.astype(F32), axis=0) * (-1.0 / ao_count)


def solution(mesh):
    in_specs = (P("tens", None, None), P("occ", None), P(), P(), P(), P())
    out_specs = P("tens", None)
    return jax.shard_map(body, mesh=mesh, in_specs=in_specs, out_specs=out_specs, check_vma=False)
```
